32 devices in a mesh: group: 4 (over z), sub: 8 (over y, x, core).
Axes of the slice: x: 2, y: 2, z: 4, core: 2. Of those that a mesh axis runs over, the one named last changes fastest.
Arguments:
- couplings: float32 [32, 6, 384, 384], P(('group', 'sub')), may hold values from -0.3125 to 0.3125
- mode_rows: float32 [49152, 128], P(('group', 'sub')), may hold values from -1.5 to 1.5
- coarse_basis: float32 [4096, 256], P(('group', 'sub')), may hold values from -0.1875 to 0.1875
- stiffness: float32 [32, 1536], P(('group', 'sub')), may hold values from 0.005 to 0.05
- own_face: int32 [32, 6], P(('group', 'sub')), may hold values from 0 to 3, as said below
- neighbour_face: int32 [32, 6], P(('group', 'sub')), may hold values from 0 to 3, as said below
- present: int32 [32, 6], P(('group', 'sub')), may hold values from 0 to 1, as said below
Outputs:
- coarse_blocks: float32 [32, 7, 128, 128], P(('group', 'sub'))
- coarse_group: float32 [4, 3, 256, 256], P('group', None, 'sub')
The draws below stay inside these ranges and needn't reach their ends.
Inputs may be any that keep to these rules, and one draw needn't show every extreme that they name: `own_face`: face block index of the subdomain's own unknowns toward each direction. Wherever present is 1, neighbour_face[d, k] equals own_face of the neighbour n(d, k) at the opposite direction (0 and 1, 2 and 3, 4 and 5 are opposite). `present`: 0 wherever the neighbour lies outside the group's plane of 4 columns and 2 rows or outside the groups, and on broken couplings; a coupling is intact on both sides or on neither.
All inputs are finite; a program needn't handle non-finite values.
Results may differ from the reference program's by a relative error of at most 0.0003.
Values sent between devices are 32-bit elements; how exact they have to be, the bound alone decides.
A program may use at most 64 MiB of HBM per device.

```python
import math
import jax
import jax.numpy as jnp
from jax import lax

BLOCK = 384
FACES = 4
UNKNOWNS = 1536
MODES = 128
MODES2 = 256
DIRS = 6
SUB_ROW = 4
SUBS = 8
GROUPS = 4
SUBDOMAINS = 32


def layout(key):
    index = jnp.arange(SUBDOMAINS, dtype=jnp.int32)
    group_of = index // SUBS
    within = index % SUBS
    row_of = within // SUB_ROW
    column = within % SUB_ROW
    faces = jax.random.randint(jax.random.fold_in(key, 11), (SUBDOMAINS, DIRS), 0, FACES, dtype=jnp.int32)
    intact = jax.random.randint(jax.random.fold_in(key, 12), (SUBDOMAINS, 3), 0, 4, dtype=jnp.int32) != 0
    upward = jnp.stack([column + 1 < SUB_ROW, row_of + 1 < SUBS // SUB_ROW, group_of + 1 < GROUPS], axis=1) & intact
    strides = jnp.array([1, SUB_ROW, SUBS], jnp.int32)
    below_index = jnp.clip(index[:, None] - strides[None, :], 0, SUBDOMAINS - 1)
    has_below = jnp.stack([column > 0, row_of > 0, group_of > 0], axis=1)
    downward = has_below & jnp.take_along_axis(upward, below_index, axis=0)
    present = jnp.stack([downward[:, 0], upward[:, 0], downward[:, 1], upward[:, 1], downward[:, 2], upward[:, 2]], axis=1).astype(jnp.int32)
    offsets = jnp.array([-1, 1, -SUB_ROW, SUB_ROW, -SUBS, SUBS], jnp.int32)
    neighbour = jnp.clip(index[:, None] + offsets[None, :], 0, SUBDOMAINS - 1)
    opposite = jnp.array([1, 0, 3, 2, 5, 4], jnp.int32)
    neighbour_faces = faces[neighbour, jnp.broadcast_to(opposite[None, :], (SUBDOMAINS, DIRS))]
    return (faces, neighbour_faces.astype(jnp.int32), present)


def draw_own_face(key, part):
    return layout(key)[0]


def draw_neighbour_face(key, part):
    return layout(key)[1]


def draw_present(key, part):
    return layout(key)[2]


def block_scale(key, extent, cuts, smallest, top_value):
    factor_of, own = 1.0, jax.random.fold_in(key, 6)
    for position, parts in cuts:
        heights = jnp.exp(jax.random.uniform(jax.random.fold_in(own, position), (parts,), jnp.float32, smallest / len(cuts), top_value / len(cuts)))
        factor_of = factor_of * jnp.repeat(heights, extent[position] // parts).reshape([-1 if axis == position else 1 for axis in range(len(extent))])
    return factor_of


def bell_draw(key, dims, scale, reach, split=(), held_as=jnp.bfloat16):
    values = scale * jax.random.normal(key, dims, jnp.float32)
    if split:
        values = values * block_scale(key, dims, split, -0.22, 0.18)
    return jnp.clip(values, -reach, reach).astype(held_as)


def setup_inputs(seed: int = 0) -> dict:
    arg_keys = jax.random.split(jax.random.key(seed), 8)
    return {
        "couplings": bell_draw(arg_keys[0], (SUBDOMAINS, DIRS, BLOCK, BLOCK), BLOCK ** -0.5, 0.3125, ((0, 32),), jnp.float32),
        "mode_rows": bell_draw(arg_keys[1], (SUBDOMAINS * UNKNOWNS, MODES), 0.25, 1.5, ((0, 32),), jnp.float32),
        "coarse_basis": bell_draw(arg_keys[2], (SUBDOMAINS * MODES, MODES2), (MODES * SUBS) ** -0.5, 0.1875, ((0, 32),), jnp.float32),
        "stiffness": jnp.clip(jnp.exp(math.log(0.05) - 2.3025851 * jax.random.uniform(arg_keys[3], (SUBDOMAINS, UNKNOWNS), jnp.float32) ** block_scale(arg_keys[3], (SUBDOMAINS, UNKNOWNS), ((0, 32),), -0.2, 0.2)), 0.005, 0.05),
        "own_face": draw_own_face(jax.random.fold_in(arg_keys[7], 71), 0),
        "neighbour_face": draw_neighbour_face(jax.random.fold_in(arg_keys[7], 71), 0),
        "present": draw_present(jax.random.fold_in(arg_keys[7], 71), 0),
    }


PRECISE = lax.Precision.HIGHEST


def matmul(left, right):
    return jnp.dot(left, right, precision=PRECISE, preferred_element_type=jnp.float32)


def transposed_product(left, right):
    return lax.dot_general(left, right, (((0,), (0,)), ((), ())), precision=PRECISE, preferred_element_type=jnp.float32)


def reference(couplings, mode_rows, coarse_basis, stiffness, own_face, neighbour_face, present):
    modes_all = mode_rows.reshape(SUBDOMAINS, UNKNOWNS, MODES)
    basis_all = coarse_basis.reshape(SUBDOMAINS, MODES, MODES2)
    offsets = jnp.array([-1, 1, -SUB_ROW, SUB_ROW, -SUBS, SUBS], jnp.int32)

    def per_subdomain(subdomain):
        own_modes = modes_all[subdomain]
        own_basis = basis_all[subdomain]
        block_list = []
        projected = []
        for direction in range(DIRS):
            neighbour = jnp.clip(subdomain + offsets[direction], 0, SUBDOMAINS - 1).astype(jnp.int32)
            own_part = lax.dynamic_slice_in_dim(own_modes, (own_face[subdomain, direction] * BLOCK).astype(jnp.int32), BLOCK, 0)
            far_part = lax.dynamic_slice_in_dim(modes_all[neighbour], (neighbour_face[subdomain, direction] * BLOCK).astype(jnp.int32), BLOCK, 0)
            weight = present[subdomain, direction].astype(jnp.float32)
            product = matmul(couplings[subdomain, direction], own_part)
            coarse_block = transposed_product(product, far_part) * weight
            block_list.append(coarse_block)
            projected.append(matmul(transposed_product(own_basis, coarse_block), basis_all[neighbour]))
        self_block = transposed_product(own_modes * stiffness[subdomain][:, None], own_modes)
        block_list.append(self_block)
        within = matmul(transposed_product(own_basis, self_block), own_basis)
        within = within + projected[0] + projected[1] + projected[2] + projected[3]
        return jnp.stack(block_list), jnp.stack([projected[4], within, projected[5]])

    blocks_out, terms_out = lax.map(per_subdomain, jnp.arange(SUBDOMAINS, dtype=jnp.int32))
    coarse_group = terms_out.reshape(GROUPS, SUBS, 3, MODES2, MODES2).sum(axis=1)
    return blocks_out, coarse_group
```

```python
import functools

import jax
import jax.numpy as jnp
from jax import lax
from jax.experimental import pallas as pl
from jax.experimental.pallas import tpu as pltpu
from jax.sharding import PartitionSpec as P

SUB_ROW = 4
F32 = jnp.float32
BF16 = jnp.bfloat16
MESH = pl.DeviceIdType.MESH


def split(value):
    high = value.astype(BF16)
    return high, (value - high.astype(F32)).astype(BF16)


def dot(left, right):
    return jnp.dot(left, right, preferred_element_type=F32)


def product(left, right):
    (lh, ll), (rh, rl) = left, right
    return dot(lh, rh) + (dot(lh, rl) + dot(ll, rh))


def bit_orders(bits):
    return (list(range(bits)), [0] + list(range(bits - 1, 0, -1)))


def block_order(order, subs):
    bits = len(order)
    return [
        sum(((p >> (bits - 1 - t)) & 1) << order[t] for t in range(bits)) for p in range(subs)
    ]


def kernel(
    groups, subs, dirs,
    own_face, present, couplings, mode_rows, coarse_basis, stiffness,
    blocks_out, group_out,
    tangent, modes, faces, far, basis, turned_hi, turned_lo, zt_hi, zt_lo, blocks, acc, got,
    load_sem, tangent_sem, out_sem, v_send, v_recv, z_send, z_recv, r_send, r_recv,
):
    block = tangent.shape[1]
    bits = subs.bit_length() - 1
    orders = bit_orders(bits)
    group, sub = lax.axis_index("group"), lax.axis_index("sub")
    column, row = sub % SUB_ROW, sub // SUB_ROW
    own = dirs

    loads = [
        pltpu.make_async_copy(mode_rows, modes, load_sem.at[0]),
        pltpu.make_async_copy(coarse_basis, basis.at[own], load_sem.at[1]),
    ]
    for load in loads:
        load.start()
    tangent_loads = [
        pltpu.make_async_copy(couplings.at[k], tangent.at[k], tangent_sem.at[k]) for k in range(dirs)
    ]
    for load in tangent_loads:
        load.start()

    has = [
        column > 0, column < SUB_ROW - 1,
        row > 0, row < subs // SUB_ROW - 1,
        group > 0, group < groups - 1,
    ]
    peers = [
        (group, sub - 1), (group, sub + 1),
        (group, sub - SUB_ROW), (group, sub + SUB_ROW),
        (group - 1, sub), (group + 1, sub),
    ]
    partners = []
    for bit in range(bits):
        mine = (sub // (1 << bit)) % 2
        partners.append((group, sub + (1 - 2 * mine) * (1 << bit)))

    barrier = pltpu.get_barrier_semaphore()
    expected = bits
    for k in range(dirs):
        expected = expected + has[k].astype(jnp.int32)

        @pl.when(has[k])
        def _(k=k):
            pl.semaphore_signal(barrier, inc=1, device_id=peers[k], device_id_type=MESH)

    for bit in range(bits):
        pl.semaphore_signal(barrier, inc=1, device_id=partners[bit], device_id_type=MESH)

    def v_copy(k, slot):
        return pltpu.make_async_remote_copy(
            src_ref=faces.at[k], dst_ref=far.at[slot], send_sem=v_send.at[k],
            recv_sem=v_recv.at[slot], device_id=peers[k], device_id_type=MESH,
        )

    def z_copy(k, slot):
        return pltpu.make_async_remote_copy(
            src_ref=basis.at[own], dst_ref=basis.at[slot], send_sem=z_send.at[k],
            recv_sem=z_recv.at[slot], device_id=peers[k], device_id_type=MESH,
        )

    sending = (4, 5, 2, 3, 0, 1)
    loads[0].wait()
    for k in sending:
        faces[k] = modes[own_face[0, k]]
    pl.semaphore_wait(barrier, expected)
    for k in sending:
        @pl.when(has[k])
        def _(k=k):
            v_copy(k, k ^ 1).start()

    loads[1].wait()
    for k in sending:
        @pl.when(has[k])
        def _(k=k):
            z_copy(k, k ^ 1).start()

        @pl.when(jnp.logical_not(has[k]))
        def _(k=k):
            far[k] = jnp.zeros(far.shape[1:], F32)
            basis[k] = jnp.zeros(basis.shape[1:], F32)

    own_basis = basis[own]
    basis_t = own_basis.T
    rows = basis_t.shape[0] // subs
    for half in range(2):
        ordered = jnp.concatenate(
            [basis_t[r * rows:(r + 1) * rows] for r in block_order(orders[half], subs)], axis=0
        )
        zt_hi[half], zt_lo[half] = split(ordered)

    all_modes = modes[...].reshape(-1, modes.shape[2])
    self_block = product(split(all_modes.T * stiffness[...]), split(all_modes))
    blocks[own] = self_block
    within = product(split(self_block), split(own_basis))

    def own_side(k, carry):
        pltpu.make_async_copy(couplings.at[k], tangent.at[k], tangent_sem.at[k]).wait()
        weight = present[0, k].astype(F32)
        value = product(split(tangent[k]), split(faces[k])) * weight
        turned_hi[k], turned_lo[k] = split(value.T)
        return carry

    lax.fori_loop(0, dirs, own_side, 0)

    for k in (0, 1, 2, 3, 4, 5):
        @pl.when(has[k])
        def _(k=k):
            v_copy(k, k).wait_recv()

        blocks[k] = product((turned_hi[k], turned_lo[k]), split(far[k]))
    blocks_copy = pltpu.make_async_copy(blocks, blocks_out, out_sem)
    blocks_copy.start()

    def projected(k):
        @pl.when(has[k])
        def _():
            z_copy(k, k).wait_recv()

        return product(split(blocks[k]), split(basis[k]))

    cols = basis.shape[2] // 2
    extent = acc[0].shape[1]

    def exchange(piece, half, t):
        bit = orders[half][t]
        mine = (sub // (1 << bit)) % 2
        length = extent // (2 << t)
        return pltpu.make_async_remote_copy(
            src_ref=acc[t].at[piece, pl.ds((1 - mine) * length, length)],
            dst_ref=got[t].at[piece], send_sem=r_send.at[t, piece], recv_sem=r_recv.at[t, piece],
            device_id=partners[bit], device_id_type=MESH,
        )

    pieces = []

    def begin(target, value):
        for half in range(2):
            piece = 2 * target + half
            part = split(value[:, half * cols:(half + 1) * cols])
            acc[0][piece] = product((zt_hi[half], zt_lo[half]), part)
            exchange(piece, half, 0).start()
            pieces.append((target, half, piece))

    begin(0, projected(4))
    begin(2, projected(5))
    for k in (0, 1, 2, 3):
        within = within + projected(k)
    begin(1, within)

    for t in range(bits):
        for target, half, piece in pieces:
            bit = orders[half][t]
            mine = (sub // (1 << bit)) % 2
            length = extent // (2 << t)
            exchange(piece, half, t).wait_recv()
            total = acc[t][piece, pl.ds(pl.multiple_of(mine * length, length), length)] + got[t][piece]
            if t < bits - 1:
                acc[t + 1][piece] = total
                exchange(piece, half, t + 1).start()
            else:
                group_out[target, :, half * cols:(half + 1) * cols] = total

    for k in sending:
        @pl.when(has[k])
        def _(k=k):
            v_copy(k, k ^ 1).wait_send()
            z_copy(k, k ^ 1).wait_send()
    for t in range(bits):
        for target, half, piece in pieces:
            exchange(piece, half, t).wait_send()
    blocks_copy.wait()


def body(groups, subs, couplings, mode_rows, coarse_basis, stiffness, own_face, neighbour_face, present):
    dirs, block = couplings.shape[1], couplings.shape[2]
    unknowns, modes = mode_rows.shape
    modes2 = coarse_basis.shape[1]
    bits = subs.bit_length() - 1
    rows = modes2 // subs
    cols = modes2 // 2
    any_space = pl.BlockSpec(memory_space=pl.ANY)
    smem = pl.BlockSpec(memory_space=pltpu.SMEM)
    vmem = pl.BlockSpec(memory_space=pltpu.VMEM)
    dma = pltpu.SemaphoreType.DMA
    work = 2 * dirs * block * modes * (block + modes) + 2 * unknowns * modes * modes
    blocks, rows_out = pl.pallas_call(
        functools.partial(kernel, groups, subs, dirs),
        out_shape=(
            jax.ShapeDtypeStruct((dirs + 1, modes, modes), F32),
            jax.ShapeDtypeStruct((3, rows, modes2), F32),
        ),
        in_specs=[smem, smem, any_space, any_space, any_space, vmem],
        out_specs=(any_space, vmem),
        scratch_shapes=[
            pltpu.VMEM((dirs, block, block), F32),
            pltpu.VMEM((unknowns // block, block, modes), F32),
            pltpu.VMEM((dirs, block, modes), F32),
            pltpu.VMEM((dirs, block, modes), F32),
            pltpu.VMEM((dirs + 1, modes, modes2), F32),
            pltpu.VMEM((dirs, modes, block), BF16),
            pltpu.VMEM((dirs, modes, block), BF16),
            pltpu.VMEM((2, modes2, modes), BF16),
            pltpu.VMEM((2, modes2, modes), BF16),
            pltpu.VMEM((dirs + 1, modes, modes), F32),
            [pltpu.VMEM((6, modes2 >> t, cols), F32) for t in range(bits)],
            [pltpu.VMEM((6, modes2 >> (t + 1), cols), F32) for t in range(bits)],
            dma((2,)), dma((dirs,)), dma,
            dma((dirs,)), dma((dirs,)), dma((dirs,)), dma((dirs,)),
            dma((bits, 6)), dma((bits, 6)),
        ],
        compiler_params=pltpu.CompilerParams(
            collective_id=0, has_side_effects=True, vmem_limit_bytes=56 * 1024 * 1024
        ),
        cost_estimate=pl.CostEstimate(
            flops=3 * work, bytes_accessed=4 * (dirs * block * block + unknowns * modes), transcendentals=0
        ),
    )(own_face, present, couplings[0], mode_rows.reshape(-1, block, modes), coarse_basis, stiffness)
    return (blocks[None], rows_out[None])


def solution(mesh):
    both = ("group", "sub")
    return jax.shard_map(
        functools.partial(body, mesh.shape["group"], mesh.shape["sub"]),
        mesh=mesh,
        in_specs=(P(both, None, None, None),) + (P(both, None),) * 6,
        out_specs=(P(both, None, None, None), P("group", None, "sub", None)),
        check_vma=False,
    )
```

```python
import functools

import jax
import jax.numpy as jnp
from jax import lax
from jax.experimental import pallas as pl
from jax.experimental.pallas import tpu as pltpu
from jax.sharding import PartitionSpec as P

SUB_ROW = 4
F32 = jnp.float32
BF16 = jnp.bfloat16
MESH = pl.DeviceIdType.MESH


def split(value):
    high = value.astype(BF16)
    return high, (value - high.astype(F32)).astype(BF16)


def dot(left, right):
    return jnp.dot(left, right, preferred_element_type=F32)


def product(left, right):
    (lh, ll), (rh, rl) = left, right
    return dot(lh, rh) + (dot(lh, rl) + dot(ll, rh))


def bit_orders(bits):
    return (list(range(bits)), [0] + list(range(bits - 1, 0, -1)))


def block_order(order, subs):
    bits = len(order)
    return [
        sum(((p >> (bits - 1 - t)) & 1) << order[t] for t in range(bits)) for p in range(subs)
    ]


def kernel(
    groups, subs, dirs,
    own_face, present, couplings, mode_rows, coarse_basis, stiffness,
    blocks_out, group_out,
    tangent, modes, faces, far, basis, turned_hi, turned_lo, zt_hi, zt_lo, blocks, acc, got,
    load_sem, tangent_sem, out_sem, v_send, v_recv, z_send, z_recv, r_send, r_recv,
):
    block = tangent.shape[1]
    bits = subs.bit_length() - 1
    orders = bit_orders(bits)
    group, sub = lax.axis_index("group"), lax.axis_index("sub")
    column, row = sub % SUB_ROW, sub // SUB_ROW
    own = dirs

    loads = [
        pltpu.make_async_copy(mode_rows, modes, load_sem.at[0]),
        pltpu.make_async_copy(coarse_basis, basis.at[own], load_sem.at[1]),
    ]
    for load in loads:
        load.start()
    tangent_loads = [
        pltpu.make_async_copy(couplings.at[k], tangent.at[k], tangent_sem.at[k]) for k in range(dirs)
    ]
    for load in tangent_loads:
        load.start()

    has = [
        column > 0, column < SUB_ROW - 1,
        row > 0, row < subs // SUB_ROW - 1,
        group > 0, group < groups - 1,
    ]
    peers = [
        (group, sub - 1), (group, sub + 1),
        (group, sub - SUB_ROW), (group, sub + SUB_ROW),
        (group - 1, sub), (group + 1, sub),
    ]
    partners = []
    for bit in range(bits):
        mine = (sub // (1 << bit)) % 2
        partners.append((group, sub + (1 - 2 * mine) * (1 << bit)))

    barrier = pltpu.get_barrier_semaphore()
    expected = bits
    for k in range(dirs):
        expected = expected + has[k].astype(jnp.int32)

        @pl.when(has[k])
        def _(k=k):
            pl.semaphore_signal(barrier, inc=1, device_id=peers[k], device_id_type=MESH)

    for bit in range(bits):
        pl.semaphore_signal(barrier, inc=1, device_id=partners[bit], device_id_type=MESH)

    def v_copy(k, slot):
        return pltpu.make_async_remote_copy(
            src_ref=faces.at[k], dst_ref=far.at[slot], send_sem=v_send.at[k],
            recv_sem=v_recv.at[slot], device_id=peers[k], device_id_type=MESH,
        )

    def z_copy(k, slot):
        return pltpu.make_async_remote_copy(
            src_ref=basis.at[own], dst_ref=basis.at[slot], send_sem=z_send.at[k],
            recv_sem=z_recv.at[slot], device_id=peers[k], device_id_type=MESH,
        )

    sending = (4, 5, 2, 3, 0, 1)
    loads[0].wait()
    for k in sending:
        faces[k] = modes[own_face[0, k]]
    pl.semaphore_wait(barrier, expected)
    for k in sending:
        @pl.when(has[k])
        def _(k=k):
            v_copy(k, k ^ 1).start()

    loads[1].wait()
    for k in sending:
        @pl.when(has[k])
        def _(k=k):
            z_copy(k, k ^ 1).start()

        @pl.when(jnp.logical_not(has[k]))
        def _(k=k):
            far[k] = jnp.zeros(far.shape[1:], F32)
            basis[k] = jnp.zeros(basis.shape[1:], F32)

    own_basis = basis[own]
    basis_t = own_basis.T
    rows = basis_t.shape[0] // subs
    for half in range(2):
        ordered = jnp.concatenate(
            [basis_t[r * rows:(r + 1) * rows] for r in block_order(orders[half], subs)], axis=0
        )
        zt_hi[half], zt_lo[half] = split(ordered)

    all_modes = modes[...].reshape(-1, modes.shape[2])
    self_block = product(split(all_modes.T * stiffness[...]), split(all_modes))
    blocks[own] = self_block
    within = product(split(self_block), split(own_basis))

    def own_side(k, carry):
        pltpu.make_async_copy(couplings.at[k], tangent.at[k], tangent_sem.at[k]).wait()
        weight = present[0, k].astype(F32)
        value = product(split(tangent[k]), split(faces[k])) * weight
        turned_hi[k], turned_lo[k] = split(value.T)
        return carry

    lax.fori_loop(0, dirs, own_side, 0)

    for k in (0, 1, 2, 3, 4, 5):
        @pl.when(has[k])
        def _(k=k):
            v_copy(k, k).wait_recv()

        blocks[k] = product((turned_hi[k], turned_lo[k]), split(far[k]))
    blocks_copy = pltpu.make_async_copy(blocks, blocks_out, out_sem)
    blocks_copy.start()

    def projected(k):
        @pl.when(has[k])
        def _():
            z_copy(k, k).wait_recv()

        return product(split(blocks[k]), split(basis[k]))

    cols = basis.shape[2] // 2
    extent = acc[0].shape[1]

    def exchange(piece, half, t):
        bit = orders[half][t]
        mine = (sub // (1 << bit)) % 2
        length = extent // (2 << t)
        return pltpu.make_async_remote_copy(
            src_ref=acc[t].at[piece, pl.ds((1 - mine) * length, length)],
            dst_ref=got[t].at[piece], send_sem=r_send.at[t, piece], recv_sem=r_recv.at[t, piece],
            device_id=partners[bit], device_id_type=MESH,
        )

    pieces = []

    def begin(target, value):
        for half in range(2):
            piece = 2 * target + half
            part = split(value[:, half * cols:(half + 1) * cols])
            acc[0][piece] = product((zt_hi[half], zt_lo[half]), part)
            exchange(piece, half, 0).start()
            pieces.append((target, half, piece))

    begin(0, projected(4))
    begin(2, projected(5))
    for k in (0, 1, 2, 3):
        within = within + projected(k)
    begin(1, within)

    for t in range(bits):
        for target, half, piece in pieces:
            bit = orders[half][t]
            mine = (sub // (1 << bit)) % 2
            length = extent // (2 << t)
            exchange(piece, half, t).wait_recv()
            total = acc[t][piece, pl.ds(pl.multiple_of(mine * length, length), length)] + got[t][piece]
            if t < bits - 1:
                acc[t + 1][piece] = total
                exchange(piece, half, t + 1).start()
            else:
                group_out[target, :, half * cols:(half + 1) * cols] = total

    for k in sending:
        @pl.when(has[k])
        def _(k=k):
            v_copy(k, k ^ 1).wait_send()
            z_copy(k, k ^ 1).wait_send()
    for t in range(bits):
        for target, half, piece in pieces:
            exchange(piece, half, t).wait_send()
    blocks_copy.wait()


def write_out(blocks, rows, blocks_out, rows_out, sem):
    copies = [
        pltpu.make_async_copy(blocks, blocks_out, sem.at[0]),
        pltpu.make_async_copy(rows, rows_out, sem.at[1]),
    ]
    for copy in copies:
        copy.start()
    for copy in copies:
        copy.wait()


def body(groups, subs, couplings, mode_rows, coarse_basis, stiffness, own_face, neighbour_face, present):
    dirs, block = couplings.shape[1], couplings.shape[2]
    unknowns, modes = mode_rows.shape
    modes2 = coarse_basis.shape[1]
    bits = subs.bit_length() - 1
    rows = modes2 // subs
    cols = modes2 // 2
    any_space = pl.BlockSpec(memory_space=pl.ANY)
    smem = pl.BlockSpec(memory_space=pltpu.SMEM)
    vmem = pl.BlockSpec(memory_space=pltpu.VMEM)
    dma = pltpu.SemaphoreType.DMA
    work = 2 * dirs * block * modes * (block + modes) + 2 * unknowns * modes * modes
    blocks, rows_out = pl.pallas_call(
        functools.partial(kernel, groups, subs, dirs),
        out_shape=(
            jax.ShapeDtypeStruct((dirs + 1, modes, modes), F32),
            jax.ShapeDtypeStruct((3, rows, modes2), F32),
        ),
        in_specs=[smem, smem, any_space, any_space, any_space, vmem],
        out_specs=(any_space, vmem),
        scratch_shapes=[
            pltpu.VMEM((dirs, block, block), F32),
            pltpu.VMEM((unknowns // block, block, modes), F32),
            pltpu.VMEM((dirs, block, modes), F32),
            pltpu.VMEM((dirs, block, modes), F32),
            pltpu.VMEM((dirs + 1, modes, modes2), F32),
            pltpu.VMEM((dirs, modes, block), BF16),
            pltpu.VMEM((dirs, modes, block), BF16),
            pltpu.VMEM((2, modes2, modes), BF16),
            pltpu.VMEM((2, modes2, modes), BF16),
            pltpu.VMEM((dirs + 1, modes, modes), F32),
            [pltpu.VMEM((6, modes2 >> t, cols), F32) for t in range(bits)],
            [pltpu.VMEM((6, modes2 >> (t + 1), cols), F32) for t in range(bits)],
            dma((2,)), dma((dirs,)), dma,
            dma((dirs,)), dma((dirs,)), dma((dirs,)), dma((dirs,)),
            dma((bits, 6)), dma((bits, 6)),
        ],
        compiler_params=pltpu.CompilerParams(
            collective_id=0, has_side_effects=True, vmem_limit_bytes=56 * 1024 * 1024
        ),
        cost_estimate=pl.CostEstimate(
            flops=3 * work, bytes_accessed=4 * (dirs * block * block + unknowns * modes), transcendentals=0
        ),
    )(own_face, present, couplings[0], mode_rows.reshape(-1, block, modes), coarse_basis, stiffness)
    blocks, rows_out = pl.pallas_call(
        write_out,
        out_shape=(
            jax.ShapeDtypeStruct(blocks.shape, F32),
            jax.ShapeDtypeStruct(rows_out.shape, F32),
        ),
        in_specs=[vmem, vmem],
        out_specs=(any_space, any_space),
        scratch_shapes=[dma((2,))],
    )(blocks, rows_out)
    return (blocks[None], rows_out[None])


def solution(mesh):
    both = ("group", "sub")
    return jax.shard_map(
        functools.partial(body, mesh.shape["group"], mesh.shape["sub"]),
        mesh=mesh,
        in_specs=(P(both, None, None, None),) + (P(both, None),) * 6,
        out_specs=(P(both, None, None, None), P("group", None, "sub", None)),
        check_vma=False,
    )
```
